32 devices in a mesh: dp: 16 (over z, x, core), tensor: 2 (over y).
Axes of the slice: x: 2, y: 2, z: 4, core: 2. Of those that a mesh axis runs over, the one named last changes fastest.
Arguments:
- tokens: bfloat16 [16384, 896], P(('dp', 'tensor')), may hold values from -6 to 6
- cotangent: bfloat16 [16384, 896], P(('dp', 'tensor')), may hold values from -6 to 6
- seq_lengths: int32 [64], replicated, may hold values from 1 to 682, as said below
- seq_place: int32 [64], replicated, may hold values from 0 to 63, as said below
- norm1_gain: float32 [896], replicated, may hold values from 0.5 to 1.5
- qkv_weight: bfloat16 [896, 1152], P(None, 'tensor'), may hold values from -0.25 to 0.25
- qkv_bias: float32 [1152], P('tensor'), may hold values from -3 to 3
- out_weight: bfloat16 [896, 896], P('tensor'), may hold values from -0.75 to 0.75
- norm2_gain: float32 [896], replicated, may hold values from 0.5 to 1.5
- gate_weight: bfloat16 [896, 4864], P(None, 'tensor'), may hold values from -0.1875 to 0.1875
- up_weight: bfloat16 [896, 4864], P(None, 'tensor'), may hold values from -0.1875 to 0.1875
- down_weight: bfloat16 [4864, 896], P('tensor'), may hold values from -0.125 to 0.125
Outputs:
- block_out: bfloat16 [16384, 896], P(('dp', 'tensor'))
- tokens_grad: float32 [16384, 896], P(('dp', 'tensor'))
- norm1_gain_grad: float32 [896], P('dp')
- qkv_weight_grad: float32 [896, 1152], P('dp', 'tensor')
- qkv_bias_grad: float32 [1152], P('tensor')
- out_weight_grad: float32 [896, 896], P('tensor', 'dp')
- norm2_gain_grad: float32 [896], P('dp')
- gate_weight_grad: float32 [896, 4864], P('dp', 'tensor')
- up_weight_grad: float32 [896, 4864], P('dp', 'tensor')
- down_weight_grad: float32 [4864, 896], P('tensor', 'dp')
The draws below stay inside these ranges and needn't reach their ends.
Inputs may be any that keep to these rules, and one draw needn't show every extreme that they name: `seq_lengths`: the lengths of the 4 sequences of one data index add up to at most 1024; some sequence has exactly 682 tokens. A permutation: sequence s lies on data index seq_place[s] // 4 with rank seq_place[s] % 4 there, so each data index holds 4 sequences.
All inputs are finite; a program needn't handle non-finite values.
Results may differ from the reference program's by a relative error of at most 0.014.
The reference program's roundings to bfloat16 on the way count: a program that leaves them out, or rounds other values in their place, can miss the bound.
Values may be sent and summed in bfloat16 or wider, within the bound.
A program may use at most 192 MiB of HBM per device.

```python
import jax
import jax.numpy as jnp
from jax import lax

D = 896
QUERY_HEADS = 14
KEY_VALUE_HEADS = 2
HEAD_WIDTH = 64
FF = 4864
CAP = 1024
SEQ_DEV = 4
MAXLEN = 682
QKV = 1152
TOKENS = 16384
SEQS = 64
N_DP = 16
N_TENSOR = 2


def layout_draw(key):
    key_perm, key_first, key_cross, key_third, key_fourth, key_pick = jax.random.split(key, 6)
    placed = jax.random.permutation(key_perm, SEQS).astype(jnp.int32)
    first_len = jax.random.randint(key_first, (N_DP,), 1, CAP // 4 + 1)
    cross_low = CAP // 2 - first_len + 1
    cross_len = jax.random.randint(key_cross, (N_DP,), cross_low, MAXLEN + 1)
    chosen = jax.random.randint(key_pick, (), 0, N_DP)
    cross_len = jnp.where(jnp.arange(N_DP) == chosen, MAXLEN, cross_len)
    remain = CAP - first_len - cross_len
    third_len = jax.random.randint(key_third, (N_DP,), 1, remain // 2 + 1)
    fourth_len = jax.random.randint(key_fourth, (N_DP,), 1, remain // 2 + 1)
    by_slot = jnp.stack([first_len, cross_len, third_len, fourth_len], axis=1).reshape(-1).astype(jnp.int32)
    return (placed, by_slot[placed])


def draw_seq_lengths(key, part):
    placed, lengths = layout_draw(key)
    return lengths.astype(jnp.int32)


def draw_seq_place(key, part):
    placed, lengths = layout_draw(key)
    return placed.astype(jnp.int32)


def spiked(entries, rng, source, target, blocks, factor):
    def block_of(dim):
        return (jnp.arange(entries.shape[dim]) // (entries.shape[dim] // blocks)).reshape((-1,) + (1,) * (entries.ndim - 1 - dim))

    one_side = jax.random.permutation(rng, blocks)[block_of(target)]
    other_side = (block_of(target) + blocks // 2) % blocks
    return jnp.where((block_of(source) == one_side) | (block_of(source) == other_side), factor * entries, entries)


def block_levels(key, extent, shards, least, high):
    level = 1.0
    for axis_at, shards_of in shards:
        steps = jax.random.uniform(jax.random.fold_in(jax.random.fold_in(key, 6), axis_at), (shards_of,), jnp.float32, least / len(shards), high / len(shards))
        level = level * jnp.repeat(jnp.exp(steps), extent[axis_at] // shards_of).reshape((-1,) + (1,) * (len(extent) - 1 - axis_at))
    return level


def centred(stream_key, dims, deviation, most, cuts=(), kind=jnp.bfloat16):
    gain = block_levels(stream_key, dims, cuts, -0.22, 0.18) if cuts else 1.0
    drawn = jax.random.normal(stream_key, dims, jnp.float32) * deviation * gain
    return jnp.minimum(jnp.maximum(drawn, -most), most).astype(kind)


def heavy_noise(key, dims, width, reach, pieces, heavy, kind=jnp.bfloat16):
    drawn = width * jax.random.normal(key, dims, jnp.float32)
    if pieces:
        drawn = drawn * block_levels(key, dims, pieces, -0.22, 0.18)
    return jnp.clip(spiked(drawn, jax.random.fold_in(key, 3), *heavy), -reach, reach).astype(kind)


def setup_inputs(seed: int = 0) -> dict:
    keys = jax.random.split(jax.random.key(seed), 13)
    return {
        "tokens": heavy_noise(keys[0], (TOKENS, D), 1.0, 6.0, ((0, 32),), (0, 1, 32, 2.75)),
        "cotangent": heavy_noise(keys[1], (TOKENS, D), 1.0, 6.0, ((0, 32),), (0, 1, 32, 2.75)),
        "seq_lengths": draw_seq_lengths(jax.random.fold_in(keys[12], 71), 0),
        "seq_place": draw_seq_place(jax.random.fold_in(keys[12], 71), 0),
        "norm1_gain": jnp.clip(1.0 + 0.1 * jax.random.normal(keys[4], (D,), jnp.float32), 0.5, 1.5),
        "qkv_weight": centred(keys[5], (D, QKV), (D // 2) ** -0.5, 0.25, ((1, 2),)),
        "qkv_bias": centred(keys[6], (QKV,), 0.5, 3.0, ((0, 2),), jnp.float32),
        "out_weight": centred(keys[7], (QUERY_HEADS * HEAD_WIDTH, D), (QUERY_HEADS * HEAD_WIDTH // 16) ** -0.5, 0.75, ((0, 2),)),
        "norm2_gain": jnp.clip(1.0 + 0.1 * jax.random.normal(keys[8], (D,), jnp.float32), 0.5, 1.5),
        "gate_weight": centred(keys[9], (D, FF), D ** -0.5, 0.1875, ((1, 2),)),
        "up_weight": centred(keys[10], (D, FF), D ** -0.5, 0.1875, ((1, 2),)),
        "down_weight": centred(keys[11], (FF, D), (FF // 2) ** -0.5, 0.125, ((0, 2),)),
    }


@jax.custom_vjp
def lower_bound(v):
    return lax.optimization_barrier(v.astype(jnp.bfloat16)).astype(jnp.float32)

@jax.custom_vjp
def low_back(v):
    return v

def low_keep(v):
    return (lower_bound(v), None)

def low_pass(kept, grad):
    return (grad,)

def back_keep(v):
    return (v, None)

def back_low(kept, grad):
    return (lower_bound(grad),)
lower_bound.defvjp(low_keep, low_pass)
low_back.defvjp(back_keep, back_low)
norm_eps = 1e-06
rope_base = 1000000.0
masked_score = -1e+30
highest = lax.Precision.HIGHEST

def seq_layout(lengths, placed, group_id, number_of_slots):
    target = group_id * SEQ_DEV + jnp.arange(SEQ_DEV, dtype=jnp.int32)
    owned = placed[None, :] == target[:, None]
    counted = lax.optimization_barrier(jnp.sum(jnp.where(owned, lengths[None, :], 0), axis=1)).astype(jnp.int32)
    seq_ends = jnp.cumsum(counted).astype(jnp.int32)
    seq_starts = seq_ends - counted
    slot_ids = jnp.arange(number_of_slots, dtype=jnp.int32)
    inside = (slot_ids[:, None] >= seq_starts[None, :]) & (slot_ids[:, None] < seq_ends[None, :])
    ranks = jnp.arange(SEQ_DEV, dtype=jnp.int32)
    segment = lax.optimization_barrier(jnp.sum(jnp.where(inside, ranks[None, :], 0), axis=1)) + jnp.where(jnp.any(inside, axis=1), 0, SEQ_DEV)
    position = slot_ids - lax.optimization_barrier(jnp.sum(jnp.where(inside, seq_starts[None, :], 0), axis=1))
    return (segment.astype(jnp.int32), position.astype(jnp.int32))

def rope_tables(position):
    half_dim = HEAD_WIDTH // 2
    inverse = jnp.power(rope_base, -2.0 * jnp.arange(half_dim, dtype=jnp.float32) / HEAD_WIDTH)
    angles = position.astype(jnp.float32)[:, None] * inverse[None, :]
    return (jnp.cos(angles), jnp.sin(angles))

def rotate(vectors, cosine, sine_table):
    half_dim = vectors.shape[-1] // 2
    first_half = vectors[..., :half_dim]
    second_half = vectors[..., half_dim:]
    return jnp.concatenate([first_half * cosine - second_half * sine_table, second_half * cosine + first_half * sine_table], axis=-1)

def allowed_keys(segment, row_start, row_end):
    query_ids = jnp.arange(row_start, row_end, dtype=jnp.int32)
    key_ids = jnp.arange(0, row_end, dtype=jnp.int32)
    query_seg = segment[row_start:row_end]
    same = query_seg[:, None] == segment[None, :row_end]
    causal = key_ids[None, :] <= query_ids[:, None]
    real_row = (query_seg[:, None] < SEQ_DEV) | (key_ids[None, :] == query_ids[:, None])
    return same & causal & real_row

def group_forward(token_rows, gain_one, w_qkv, b_qkv, w_out, gain_two, w_gate, w_up, w_down, segment, position):
    number_of_slots = token_rows.shape[0]
    rms_one = lax.rsqrt(lax.optimization_barrier(jnp.mean(token_rows * token_rows, axis=-1, keepdims=True)) + norm_eps)
    normed_one = lower_bound(token_rows * rms_one * gain_one)
    projected = low_back(jnp.dot(normed_one, w_qkv, precision=highest) + b_qkv)
    per_partition = projected.reshape(number_of_slots, N_TENSOR, -1)
    query_columns = QUERY_HEADS // N_TENSOR * HEAD_WIDTH
    key_columns = KEY_VALUE_HEADS // N_TENSOR * HEAD_WIDTH
    query_rows = per_partition[:, :, :query_columns].reshape(number_of_slots, KEY_VALUE_HEADS, QUERY_HEADS // KEY_VALUE_HEADS, HEAD_WIDTH)
    key_matrix = per_partition[:, :, query_columns:query_columns + key_columns].reshape(number_of_slots, KEY_VALUE_HEADS, HEAD_WIDTH)
    value_matrix = lower_bound(per_partition[:, :, query_columns + key_columns:].reshape(number_of_slots, KEY_VALUE_HEADS, HEAD_WIDTH))
    cosine, sine_table = rope_tables(position)
    queries_r = lower_bound(rotate(query_rows, cosine[:, None, None, :], sine_table[:, None, None, :]))
    keys_r = lower_bound(rotate(key_matrix, cosine[:, None, :], sine_table[:, None, :]))
    scores = low_back(jnp.einsum('qjgd,kjd->jgqk', queries_r, keys_r, precision=highest) * HEAD_WIDTH ** (-0.5))
    key_mask = allowed_keys(segment, 0, number_of_slots)
    scores = jnp.where(key_mask[None, None], scores, masked_score)
    attn_probs = lower_bound(jax.nn.softmax(scores, axis=-1))
    context = jnp.einsum('jgqk,kjd->qjgd', attn_probs, value_matrix, precision=highest).reshape(number_of_slots, QUERY_HEADS * HEAD_WIDTH)
    context = lower_bound(low_back(context))
    hidden_one = token_rows + low_back(jnp.dot(context, w_out, precision=highest))
    rms_two = lax.rsqrt(lax.optimization_barrier(jnp.mean(hidden_one * hidden_one, axis=-1, keepdims=True)) + norm_eps)
    normed_two = lower_bound(hidden_one * rms_two * gain_two)
    gate_pre = low_back(jnp.dot(normed_two, w_gate, precision=highest))
    up_pre = low_back(jnp.dot(normed_two, w_up, precision=highest))
    mixed = lower_bound(jax.nn.silu(gate_pre) * up_pre)
    return hidden_one + jnp.dot(mixed, w_down, precision=highest)

def reference(tokens, cotangent, seq_lengths, seq_place, norm1_gain, qkv_weight, qkv_bias, out_weight, norm2_gain, gate_weight, up_weight, down_weight):
    weights = tuple((item.astype(jnp.float32) for item in (norm1_gain, qkv_weight, qkv_bias, out_weight, norm2_gain, gate_weight, up_weight, down_weight)))
    token_groups = tokens.reshape(N_DP, CAP, D)
    cot_groups = cotangent.reshape(N_DP, CAP, D)
    zero_grads = tuple((jnp.zeros_like(item) for item in weights))

    def group_step(totals, inputs_now):
        group_id, token_rows, cot_rows = inputs_now
        segment, position = seq_layout(seq_lengths, seq_place, group_id, CAP)

        def forward(rows_f, *params):
            return group_forward(rows_f, *params, segment, position)
        result, pullback = jax.vjp(forward, token_rows.astype(jnp.float32), *weights)
        gradients = pullback(cot_rows.astype(jnp.float32))
        totals = tuple((total + grad for total, grad in zip(totals, gradients[1:])))
        return (totals, (result.astype(jnp.bfloat16), gradients[0]))
    totals, (results, token_grads) = lax.scan(group_step, zero_grads, (jnp.arange(N_DP, dtype=jnp.int32), token_groups, cot_groups))
    return (results.reshape(TOKENS, D), token_grads.reshape(TOKENS, D), totals[0], totals[1], totals[2], totals[3], totals[4], totals[5], totals[6], totals[7])
```

```python
import jax
import jax.numpy as jnp
from jax import lax
from jax.sharding import PartitionSpec as P

QUERY_HEADS = 14
KEY_VALUE_HEADS = 2
HEAD_WIDTH = 64
SEQ_DEV = 4
QB = 512


norm_eps = 1e-06
rope_base = 1000000.0
masked_score = -1e30


def seq_layout(lengths, placed, group_id, number_of_slots):
    target = group_id * SEQ_DEV + jnp.arange(SEQ_DEV, dtype=jnp.int32)
    owned = placed[None, :] == target[:, None]
    counted = jnp.sum(jnp.where(owned, lengths[None, :], 0), axis=1)
    seq_ends = jnp.cumsum(counted)
    seq_starts = seq_ends - counted
    slot_ids = jnp.arange(number_of_slots, dtype=jnp.int32)
    inside = (slot_ids[:, None] >= seq_starts[None, :]) & (slot_ids[:, None] < seq_ends[None, :])
    ranks = jnp.arange(SEQ_DEV, dtype=jnp.int32)
    segment = jnp.sum(jnp.where(inside, ranks[None, :], 0), axis=1) + jnp.where(
        jnp.any(inside, axis=1), 0, SEQ_DEV
    )
    position = slot_ids - jnp.sum(jnp.where(inside, seq_starts[None, :], 0), axis=1)
    return (segment, position)


def rope_tables(position):
    half_dim = HEAD_WIDTH // 2
    inverse = jnp.power(rope_base, -2.0 * jnp.arange(half_dim, dtype=jnp.float32) / HEAD_WIDTH)
    angles = position.astype(jnp.float32)[:, None] * inverse[None, :]
    return (jnp.cos(angles), jnp.sin(angles))


def rotate(vectors, cosine, sine_table):
    half_dim = vectors.shape[-1] // 2
    first_half = vectors[..., :half_dim]
    second_half = vectors[..., half_dim:]
    return jnp.concatenate(
        [
            first_half * cosine - second_half * sine_table,
            second_half * cosine + first_half * sine_table,
        ],
        axis=-1,
    )


def rotate_back(vectors, cosine, sine_table):
    half_dim = vectors.shape[-1] // 2
    first_half = vectors[..., :half_dim]
    second_half = vectors[..., half_dim:]
    return jnp.concatenate(
        [
            first_half * cosine + second_half * sine_table,
            second_half * cosine - first_half * sine_table,
        ],
        axis=-1,
    )


def allowed_keys(segment, row_start, row_end):
    query_ids = jnp.arange(row_start, row_end, dtype=jnp.int32)
    key_ids = jnp.arange(0, row_end, dtype=jnp.int32)
    query_seg = segment[row_start:row_end]
    same = query_seg[:, None] == segment[None, :row_end]
    causal = key_ids[None, :] <= query_ids[:, None]
    real_row = (query_seg[:, None] < SEQ_DEV) | (key_ids[None, :] == query_ids[:, None])
    return same & causal & real_row


def rms_forward(token_rows, gain):
    rms_scale = lax.rsqrt(jnp.mean(token_rows * token_rows, axis=-1, keepdims=True) + norm_eps)
    return (rms_scale, token_rows * rms_scale * gain)


def rms_backward(token_rows, rms_scale, gain, grad_rows):
    weighted = gain * grad_rows
    inner = jnp.mean(weighted * token_rows, axis=-1, keepdims=True)
    row_grad = rms_scale * weighted - token_rows * (rms_scale * rms_scale * rms_scale) * inner
    gain_grad = jnp.sum(grad_rows * token_rows * rms_scale, axis=0)
    return (row_grad, gain_grad)


def contract_rows(left, right):
    return lax.dot_general(
        left, right, (((0,), (0,)), ((), ())), preferred_element_type=jnp.float32
    )


def times_transpose(left, right):
    return lax.dot_general(
        left, right, (((1,), (1,)), ((), ())), preferred_element_type=jnp.float32
    )


def pair_swap(block):
    return lax.ppermute(block, "tensor", [(0, 1), (1, 0)])


def gather_pair(own):
    other = pair_swap(own)
    first = lax.axis_index("tensor") == 0
    return jnp.concatenate(
        [jnp.where(first, own, other), jnp.where(first, other, own)], axis=0
    )


def half_rows(array, which):
    rows = array.shape[0] // 2
    return lax.dynamic_slice_in_dim(array, which * rows, rows, axis=0)


def sum_pair(partial_of):
    me = lax.axis_index("tensor")
    sent = pair_swap(partial_of(1 - me).astype(jnp.bfloat16))
    return partial_of(me) + sent.astype(jnp.float32)


def dp_sum_rows(partial):
    count = lax.axis_size("dp")
    me = lax.axis_index("dp")
    rows = partial.shape[0] // count
    current = partial.reshape(count, rows, partial.shape[1])
    step = 1
    while step < count:
        bit = (me // step) % 2
        pairs = current.reshape(current.shape[0] // 2, 2, rows, partial.shape[1])
        sent = lax.dynamic_index_in_dim(pairs, 1 - bit, axis=1, keepdims=False)
        kept = lax.dynamic_index_in_dim(pairs, bit, axis=1, keepdims=False)
        got = lax.ppermute(sent, "dp", [(i, i ^ step) for i in range(count)])
        current = kept.astype(jnp.float32) + got.astype(jnp.float32)
        step *= 2
        if step < count:
            current = current.astype(jnp.bfloat16)
    return current[0]


def shards(
    tokens,
    cotangent,
    seq_lengths,
    seq_place,
    norm1_gain,
    qkv_weight,
    qkv_bias,
    out_weight,
    norm2_gain,
    gate_weight,
    up_weight,
    down_weight,
):
    local_rows = tokens.shape[0]
    group_rows = local_rows * lax.axis_size("tensor")
    segment, position = seq_layout(seq_lengths, seq_place, lax.axis_index("dp"), group_rows)
    query_columns = out_weight.shape[0]
    key_columns = (qkv_weight.shape[1] - query_columns) // 2
    kv_local = key_columns // HEAD_WIDTH
    heads_per_group = QUERY_HEADS // KEY_VALUE_HEADS
    score_scale = HEAD_WIDTH ** (-0.5)
    block_count = group_rows // QB
    token_vals = tokens.astype(jnp.float32)
    rms_one, normed_one = rms_forward(token_vals, norm1_gain)
    normed_one = gather_pair(normed_one.astype(jnp.bfloat16))
    cot_sent, _ = lax.optimization_barrier((cotangent, normed_one))
    cot_group = gather_pair(cot_sent)
    d_mixed = lax.optimization_barrier(times_transpose(cot_group, down_weight))
    projected = jnp.dot(normed_one, qkv_weight, preferred_element_type=jnp.float32) + qkv_bias
    query_rows = projected[:, :query_columns].reshape(
        group_rows, kv_local, heads_per_group, HEAD_WIDTH
    )
    key_matrix = projected[:, query_columns : query_columns + key_columns].reshape(
        group_rows, kv_local, HEAD_WIDTH
    )
    value_matrix = (
        projected[:, query_columns + key_columns :]
        .reshape(group_rows, kv_local, HEAD_WIDTH)
        .astype(jnp.bfloat16)
    )
    cosine, sine_table = rope_tables(position)
    queries_r = rotate(query_rows, cosine[:, None, None, :], sine_table[:, None, None, :]).astype(
        jnp.bfloat16
    )
    keys_r = rotate(key_matrix, cosine[:, None, :], sine_table[:, None, :]).astype(jnp.bfloat16)
    key_masks = []
    log_totals = []
    contexts = []
    for block_id in range(block_count):
        row_start = block_id * QB
        row_end = row_start + QB
        key_mask = allowed_keys(segment, row_start, row_end)
        scores = (
            jnp.einsum(
                "qjgd,kjd->jgqk",
                queries_r[row_start:row_end],
                keys_r[:row_end],
                preferred_element_type=jnp.float32,
            )
            * score_scale
        )
        scores = jnp.where(key_mask[None, None], scores, masked_score)
        row_max = jnp.max(scores, axis=-1, keepdims=True)
        expo = jnp.exp(scores - row_max)
        row_total = jnp.sum(expo, axis=-1, keepdims=True)
        attn_probs = (expo / row_total).astype(jnp.bfloat16)
        key_masks.append(key_mask)
        log_totals.append(row_max + jnp.log(row_total))
        contexts.append(
            jnp.einsum(
                "jgqk,kjd->qjgd",
                attn_probs,
                value_matrix[:row_end],
                preferred_element_type=jnp.float32,
            )
        )
    context = (
        jnp.concatenate(contexts, axis=0).reshape(group_rows, query_columns).astype(jnp.bfloat16)
    )
    hidden_one = token_vals + sum_pair(
        lambda t: jnp.dot(half_rows(context, t), out_weight, preferred_element_type=jnp.float32)
    )
    rms_two, normed_two = rms_forward(hidden_one, norm2_gain)
    normed_two = gather_pair(normed_two.astype(jnp.bfloat16))
    gate_pre = jnp.dot(normed_two, gate_weight, preferred_element_type=jnp.float32)
    up_pre = jnp.dot(normed_two, up_weight, preferred_element_type=jnp.float32)
    activated = jax.nn.silu(gate_pre)
    mixed = (activated * up_pre).astype(jnp.bfloat16)
    block_result = (
        hidden_one
        + sum_pair(
            lambda t: jnp.dot(half_rows(mixed, t), down_weight, preferred_element_type=jnp.float32)
        )
    ).astype(jnp.bfloat16)
    down_grad = contract_rows(cot_group, mixed).astype(jnp.bfloat16)
    sigmoid_gate = jax.nn.sigmoid(gate_pre)
    d_gate = (d_mixed * up_pre * sigmoid_gate * (1.0 + gate_pre * (1.0 - sigmoid_gate))).astype(
        jnp.bfloat16
    )
    d_up = (d_mixed * activated).astype(jnp.bfloat16)
    gate_grad = contract_rows(normed_two, d_gate).astype(jnp.bfloat16)
    up_grad = contract_rows(normed_two, d_up).astype(jnp.bfloat16)
    d_normed_two = sum_pair(
        lambda t: times_transpose(half_rows(d_gate, t), gate_weight)
        + times_transpose(half_rows(d_up, t), up_weight)
    )
    d_hidden_norm, gain_two_grad = rms_backward(hidden_one, rms_two, norm2_gain, d_normed_two)
    d_hidden = cotangent.astype(jnp.float32) + d_hidden_norm
    d_resid = gather_pair(d_hidden.astype(jnp.bfloat16))
    out_grad = contract_rows(d_resid, context).astype(jnp.bfloat16)
    d_context = (
        times_transpose(d_resid, out_weight)
        .astype(jnp.bfloat16)
        .reshape(group_rows, kv_local, heads_per_group, HEAD_WIDTH)
    )
    d_query_blocks = []
    d_keys = jnp.zeros((group_rows, kv_local, HEAD_WIDTH), jnp.float32)
    d_values = jnp.zeros((group_rows, kv_local, HEAD_WIDTH), jnp.float32)
    for block_id in range(block_count):
        row_start = block_id * QB
        row_end = row_start + QB
        scores = (
            jnp.einsum(
                "qjgd,kjd->jgqk",
                queries_r[row_start:row_end],
                keys_r[:row_end],
                preferred_element_type=jnp.float32,
            )
            * score_scale
        )
        scores = jnp.where(key_masks[block_id][None, None], scores, masked_score)
        probs_full = jnp.exp(scores - log_totals[block_id])
        attn_probs = probs_full.astype(jnp.bfloat16)
        d_block = d_context[row_start:row_end]
        d_probs = jnp.einsum(
            "qjgd,kjd->jgqk", d_block, value_matrix[:row_end], preferred_element_type=jnp.float32
        )
        inner = jnp.sum(probs_full * d_probs, axis=-1, keepdims=True)
        d_scores = (probs_full * (d_probs - inner)).astype(jnp.bfloat16)
        d_query_blocks.append(
            jnp.einsum(
                "jgqk,kjd->qjgd", d_scores, keys_r[:row_end], preferred_element_type=jnp.float32
            )
            * score_scale
        )
        d_keys = d_keys.at[:row_end].add(
            jnp.einsum(
                "jgqk,qjgd->kjd",
                d_scores,
                queries_r[row_start:row_end],
                preferred_element_type=jnp.float32,
            )
            * score_scale
        )
        d_values = d_values.at[:row_end].add(
            jnp.einsum("jgqk,qjgd->kjd", attn_probs, d_block, preferred_element_type=jnp.float32)
        )
    d_queries = rotate_back(
        jnp.concatenate(d_query_blocks, axis=0),
        cosine[:, None, None, :],
        sine_table[:, None, None, :],
    )
    d_keys = rotate_back(d_keys, cosine[:, None, :], sine_table[:, None, :])
    d_proj = jnp.concatenate(
        [
            d_queries.reshape(group_rows, query_columns),
            d_keys.reshape(group_rows, key_columns),
            d_values.reshape(group_rows, key_columns),
        ],
        axis=1,
    ).astype(jnp.bfloat16)
    qkv_grad = contract_rows(normed_one, d_proj).astype(jnp.bfloat16)
    bias_grad = jnp.sum(d_proj, axis=0, dtype=jnp.float32)
    d_normed_one = sum_pair(lambda t: times_transpose(half_rows(d_proj, t), qkv_weight))
    d_token_norm, gain_one_grad = rms_backward(token_vals, rms_one, norm1_gain, d_normed_one)
    tokens_grad = d_hidden + d_token_norm
    down_grad = dp_sum_rows(down_grad).T
    gate_grad = dp_sum_rows(gate_grad)
    up_grad = dp_sum_rows(up_grad)
    small = dp_sum_rows(jnp.concatenate([qkv_grad, out_grad], axis=1))
    qkv_grad = small[:, : qkv_weight.shape[1]]
    out_grad = small[:, qkv_weight.shape[1] :].T
    me = lax.axis_index("tensor")
    width = norm1_gain.shape[0]
    bias_columns = bias_grad.shape[0]
    placed_bias = lax.dynamic_update_slice_in_dim(
        jnp.zeros((bias_columns * lax.axis_size("tensor"),), jnp.float32),
        bias_grad,
        me * bias_columns,
        axis=0,
    )
    sums = lax.psum(
        jnp.concatenate([gain_one_grad, gain_two_grad, placed_bias]), ("dp", "tensor")
    )
    share = width // lax.axis_size("dp")
    gain_at = lax.axis_index("dp") * share
    gain_one_grad = lax.dynamic_slice_in_dim(sums, gain_at, share)
    gain_two_grad = lax.dynamic_slice_in_dim(sums, width + gain_at, share)
    bias_grad = lax.dynamic_slice_in_dim(sums, 2 * width + me * bias_columns, bias_columns)
    return (
        block_result,
        tokens_grad,
        gain_one_grad,
        qkv_grad,
        bias_grad,
        out_grad,
        gain_two_grad,
        gate_grad,
        up_grad,
        down_grad,
    )


def solution(mesh):
    in_specs = (
        P(("dp", "tensor"), None),
        P(("dp", "tensor"), None),
        P(),
        P(),
        P(),
        P(None, "tensor"),
        P("tensor"),
        P("tensor", None),
        P(),
        P(None, "tensor"),
        P(None, "tensor"),
        P("tensor", None),
    )
    out_specs = (
        P(("dp", "tensor"), None),
        P(("dp", "tensor"), None),
        P("dp"),
        P("dp", "tensor"),
        P("tensor"),
        P("tensor", "dp"),
        P("dp"),
        P("dp", "tensor"),
        P("dp", "tensor"),
        P("tensor", "dp"),
    )
    return jax.shard_map(shards, mesh=mesh, in_specs=in_specs, out_specs=out_specs, check_vma=False)
```

```python
import jax
import jax.numpy as jnp
from jax import lax
from jax.sharding import PartitionSpec as P

QUERY_HEADS = 14
KEY_VALUE_HEADS = 2
HEAD_WIDTH = 64
SEQ_DEV = 4
QB = 512


norm_eps = 1e-06
rope_base = 1000000.0
masked_score = -1e30


def seq_layout(lengths, placed, group_id, number_of_slots):
    target = group_id * SEQ_DEV + jnp.arange(SEQ_DEV, dtype=jnp.int32)
    owned = placed[None, :] == target[:, None]
    counted = jnp.sum(jnp.where(owned, lengths[None, :], 0), axis=1)
    seq_ends = jnp.cumsum(counted)
    seq_starts = seq_ends - counted
    slot_ids = jnp.arange(number_of_slots, dtype=jnp.int32)
    inside = (slot_ids[:, None] >= seq_starts[None, :]) & (slot_ids[:, None] < seq_ends[None, :])
    ranks = jnp.arange(SEQ_DEV, dtype=jnp.int32)
    segment = jnp.sum(jnp.where(inside, ranks[None, :], 0), axis=1) + jnp.where(
        jnp.any(inside, axis=1), 0, SEQ_DEV
    )
    position = slot_ids - jnp.sum(jnp.where(inside, seq_starts[None, :], 0), axis=1)
    return (segment, position)


def rope_tables(position):
    half_dim = HEAD_WIDTH // 2
    inverse = jnp.power(rope_base, -2.0 * jnp.arange(half_dim, dtype=jnp.float32) / HEAD_WIDTH)
    angles = position.astype(jnp.float32)[:, None] * inverse[None, :]
    return (jnp.cos(angles), jnp.sin(angles))


def rotate(vectors, cosine, sine_table):
    half_dim = vectors.shape[-1] // 2
    first_half = vectors[..., :half_dim]
    second_half = vectors[..., half_dim:]
    return jnp.concatenate(
        [
            first_half * cosine - second_half * sine_table,
            second_half * cosine + first_half * sine_table,
        ],
        axis=-1,
    )


def rotate_back(vectors, cosine, sine_table):
    half_dim = vectors.shape[-1] // 2
    first_half = vectors[..., :half_dim]
    second_half = vectors[..., half_dim:]
    return jnp.concatenate(
        [
            first_half * cosine + second_half * sine_table,
            second_half * cosine - first_half * sine_table,
        ],
        axis=-1,
    )


def allowed_keys(segment, row_start, row_end):
    query_ids = jnp.arange(row_start, row_end, dtype=jnp.int32)
    key_ids = jnp.arange(0, row_end, dtype=jnp.int32)
    query_seg = segment[row_start:row_end]
    same = query_seg[:, None] == segment[None, :row_end]
    causal = key_ids[None, :] <= query_ids[:, None]
    real_row = (query_seg[:, None] < SEQ_DEV) | (key_ids[None, :] == query_ids[:, None])
    return same & causal & real_row


def rms_forward(token_rows, gain):
    rms_scale = lax.rsqrt(jnp.mean(token_rows * token_rows, axis=-1, keepdims=True) + norm_eps)
    return (rms_scale, token_rows * rms_scale * gain)


def rms_backward(token_rows, rms_scale, gain, grad_rows):
    weighted = gain * grad_rows
    inner = jnp.mean(weighted * token_rows, axis=-1, keepdims=True)
    row_grad = rms_scale * weighted - token_rows * (rms_scale * rms_scale * rms_scale) * inner
    gain_grad = jnp.sum(grad_rows * token_rows * rms_scale, axis=0)
    return (row_grad, gain_grad)


def contract_rows(left, right):
    return lax.dot_general(
        left, right, (((0,), (0,)), ((), ())), preferred_element_type=jnp.float32
    )


def times_transpose(left, right):
    return lax.dot_general(
        left, right, (((1,), (1,)), ((), ())), preferred_element_type=jnp.float32
    )


def pair_swap(block):
    return lax.ppermute(block, "tensor", [(0, 1), (1, 0)])


def gather_pair(own):
    other = pair_swap(own)
    first = lax.axis_index("tensor") == 0
    return jnp.concatenate(
        [jnp.where(first, own, other), jnp.where(first, other, own)], axis=0
    )


def half_rows(array, which):
    rows = array.shape[0] // 2
    return lax.dynamic_slice_in_dim(array, which * rows, rows, axis=0)


def sum_pair(partial_of):
    me = lax.axis_index("tensor")
    sent = pair_swap(partial_of(1 - me).astype(jnp.bfloat16))
    return partial_of(me) + sent.astype(jnp.float32)


def dp_bits(last_first):
    count = lax.axis_size("dp")
    bits = []
    step = 1
    while step < count:
        bits.append(step)
        step *= 2
    if last_first:
        bits = bits[:1] + bits[2:] + bits[1:2]
    return bits


def dp_blocks(partial):
    count = lax.axis_size("dp")
    return partial.reshape(count, partial.shape[0] // count, partial.shape[1])


def dp_stage(current, bits, at):
    count = lax.axis_size("dp")
    step = bits[at]
    low = 2 ** sum(1 for later in bits[at + 1 :] if later < step)
    blocks, rows, columns = current.shape
    bit = (lax.axis_index("dp") // step) % 2
    pairs = current.reshape(blocks // (2 * low), 2, low, rows, columns)
    sent = lax.dynamic_index_in_dim(pairs, 1 - bit, axis=1, keepdims=False)
    kept = lax.dynamic_index_in_dim(pairs, bit, axis=1, keepdims=False)
    sent = sent.reshape(blocks // 2, rows, columns)
    kept = kept.reshape(blocks // 2, rows, columns)
    got = lax.ppermute(sent, "dp", [(i, i ^ step) for i in range(count)])
    total = kept.astype(jnp.float32) + got.astype(jnp.float32)
    return total if at == len(bits) - 1 else total.astype(jnp.bfloat16)


def dp_rest(current, bits, at):
    while at < len(bits):
        current = dp_stage(current, bits, at)
        at += 1
    return current[0]


def after(value, *earlier):
    return lax.optimization_barrier((value,) + earlier)


def shards(
    tokens,
    cotangent,
    seq_lengths,
    seq_place,
    norm1_gain,
    qkv_weight,
    qkv_bias,
    out_weight,
    norm2_gain,
    gate_weight,
    up_weight,
    down_weight,
):
    local_rows = tokens.shape[0]
    group_rows = local_rows * lax.axis_size("tensor")
    segment, position = seq_layout(seq_lengths, seq_place, lax.axis_index("dp"), group_rows)
    query_columns = out_weight.shape[0]
    key_columns = (qkv_weight.shape[1] - query_columns) // 2
    kv_local = key_columns // HEAD_WIDTH
    heads_per_group = QUERY_HEADS // KEY_VALUE_HEADS
    score_scale = HEAD_WIDTH ** (-0.5)
    block_count = group_rows // QB
    token_vals = tokens.astype(jnp.float32)
    rms_one, normed_one = rms_forward(token_vals, norm1_gain)
    normed_one = gather_pair(normed_one.astype(jnp.bfloat16))
    cot_sent, _ = lax.optimization_barrier((cotangent, normed_one))
    cot_group = gather_pair(cot_sent)
    projected = jnp.dot(normed_one, qkv_weight, preferred_element_type=jnp.float32) + qkv_bias
    query_rows = projected[:, :query_columns].reshape(
        group_rows, kv_local, heads_per_group, HEAD_WIDTH
    )
    key_matrix = projected[:, query_columns : query_columns + key_columns].reshape(
        group_rows, kv_local, HEAD_WIDTH
    )
    value_matrix = (
        projected[:, query_columns + key_columns :]
        .reshape(group_rows, kv_local, HEAD_WIDTH)
        .astype(jnp.bfloat16)
    )
    cosine, sine_table = rope_tables(position)
    queries_r = rotate(query_rows, cosine[:, None, None, :], sine_table[:, None, None, :]).astype(
        jnp.bfloat16
    )
    keys_r = rotate(key_matrix, cosine[:, None, :], sine_table[:, None, :]).astype(jnp.bfloat16)
    key_masks = []
    log_totals = []
    contexts = []
    for block_id in range(block_count):
        row_start = block_id * QB
        row_end = row_start + QB
        key_mask = allowed_keys(segment, row_start, row_end)
        scores = (
            jnp.einsum(
                "qjgd,kjd->jgqk",
                queries_r[row_start:row_end],
                keys_r[:row_end],
                preferred_element_type=jnp.float32,
            )
            * score_scale
        )
        scores = jnp.where(key_mask[None, None], scores, masked_score)
        row_max = jnp.max(scores, axis=-1, keepdims=True)
        expo = jnp.exp(scores - row_max)
        row_total = jnp.sum(expo, axis=-1, keepdims=True)
        attn_probs = (expo / row_total).astype(jnp.bfloat16)
        key_masks.append(key_mask)
        log_totals.append(row_max + jnp.log(row_total))
        contexts.append(
            jnp.einsum(
                "jgqk,kjd->qjgd",
                attn_probs,
                value_matrix[:row_end],
                preferred_element_type=jnp.float32,
            )
        )
    context = (
        jnp.concatenate(contexts, axis=0).reshape(group_rows, query_columns).astype(jnp.bfloat16)
    )
    context, cot_group = after(context, cot_group)
    hidden_one = token_vals + sum_pair(
        lambda t: jnp.dot(half_rows(context, t), out_weight, preferred_element_type=jnp.float32)
    )
    rms_two, normed_two = rms_forward(hidden_one, norm2_gain)
    d_mixed = times_transpose(cot_group, down_weight)
    normed_two, d_mixed = after(gather_pair(normed_two.astype(jnp.bfloat16)), d_mixed)
    gate_pre = jnp.dot(normed_two, gate_weight, preferred_element_type=jnp.float32)
    up_pre = jnp.dot(normed_two, up_weight, preferred_element_type=jnp.float32)
    activated = jax.nn.silu(gate_pre)
    mixed = (activated * up_pre).astype(jnp.bfloat16)
    sigmoid_gate = jax.nn.sigmoid(gate_pre)
    d_gate = (d_mixed * up_pre * sigmoid_gate * (1.0 + gate_pre * (1.0 - sigmoid_gate))).astype(
        jnp.bfloat16
    )
    d_up = (d_mixed * activated).astype(jnp.bfloat16)
    me = lax.axis_index("tensor")
    other_part = (
        times_transpose(half_rows(d_gate, 1 - me), gate_weight)
        + times_transpose(half_rows(d_up, 1 - me), up_weight)
    ).astype(jnp.bfloat16)
    d_normed_sent = pair_swap(other_part)
    mixed, d_gate, d_up, other_part = after(mixed, d_gate, d_up, other_part)
    own_part = times_transpose(half_rows(d_gate, me), gate_weight) + times_transpose(
        half_rows(d_up, me), up_weight
    )
    down_grad = contract_rows(cot_group, mixed).astype(jnp.bfloat16)
    gate_grad = contract_rows(normed_two, d_gate).astype(jnp.bfloat16)
    own_part, d_normed_sent, down_grad, gate_grad = after(
        own_part, d_normed_sent, down_grad, gate_grad
    )
    d_normed_two = own_part + d_normed_sent.astype(jnp.float32)
    bits_x = dp_bits(False)
    bits_z = dp_bits(True)
    down_sum = dp_stage(dp_blocks(down_grad), bits_x, 0)
    gate_sum = dp_stage(dp_blocks(gate_grad), bits_z, 0)
    d_hidden_norm, gain_two_grad = rms_backward(hidden_one, rms_two, norm2_gain, d_normed_two)
    d_hidden = cotangent.astype(jnp.float32) + d_hidden_norm
    d_resid_own = d_hidden.astype(jnp.bfloat16)
    d_up, mixed, d_resid_own = after(d_up, mixed, d_resid_own)
    d_resid = gather_pair(d_resid_own)
    up_grad = contract_rows(normed_two, d_up).astype(jnp.bfloat16)
    block_sent = jnp.dot(
        half_rows(mixed, 1 - me), down_weight, preferred_element_type=jnp.float32
    ).astype(jnp.bfloat16)
    block_own = jnp.dot(half_rows(mixed, me), down_weight, preferred_element_type=jnp.float32)
    d_resid, up_grad, block_sent, block_own, down_sum, gate_sum = after(
        d_resid, up_grad, block_sent, block_own, down_sum, gate_sum
    )
    up_sum = dp_stage(dp_blocks(up_grad), bits_x, 0)
    down_sum = dp_stage(down_sum, bits_x, 1)
    gate_sum = dp_stage(gate_sum, bits_z, 1)
    block_result = (hidden_one + (block_own + pair_swap(block_sent).astype(jnp.float32))).astype(
        jnp.bfloat16
    )
    out_grad = contract_rows(d_resid, context).astype(jnp.bfloat16)
    d_context = (
        times_transpose(d_resid, out_weight)
        .astype(jnp.bfloat16)
        .reshape(group_rows, kv_local, heads_per_group, HEAD_WIDTH)
    )
    d_query_blocks = []
    d_keys = jnp.zeros((group_rows, kv_local, HEAD_WIDTH), jnp.float32)
    d_values = jnp.zeros((group_rows, kv_local, HEAD_WIDTH), jnp.float32)
    for block_id in range(block_count):
        row_start = block_id * QB
        row_end = row_start + QB
        scores = (
            jnp.einsum(
                "qjgd,kjd->jgqk",
                queries_r[row_start:row_end],
                keys_r[:row_end],
                preferred_element_type=jnp.float32,
            )
            * score_scale
        )
        scores = jnp.where(key_masks[block_id][None, None], scores, masked_score)
        probs_full = jnp.exp(scores - log_totals[block_id])
        attn_probs = probs_full.astype(jnp.bfloat16)
        d_block = d_context[row_start:row_end]
        d_probs = jnp.einsum(
            "qjgd,kjd->jgqk", d_block, value_matrix[:row_end], preferred_element_type=jnp.float32
        )
        inner = jnp.sum(probs_full * d_probs, axis=-1, keepdims=True)
        d_scores = (probs_full * (d_probs - inner)).astype(jnp.bfloat16)
        d_query_blocks.append(
            jnp.einsum(
                "jgqk,kjd->qjgd", d_scores, keys_r[:row_end], preferred_element_type=jnp.float32
            )
            * score_scale
        )
        if block_id == 0:
            d_scores, d_context, up_sum, down_sum, gate_sum, block_result = after(
                d_scores, d_context, up_sum, down_sum, gate_sum, block_result
            )
            up_sum = dp_stage(up_sum, bits_x, 1)
            down_sum = dp_stage(down_sum, bits_x, 2)
            gate_sum = dp_stage(gate_sum, bits_z, 2)
        d_keys = d_keys.at[:row_end].add(
            jnp.einsum(
                "jgqk,qjgd->kjd",
                d_scores,
                queries_r[row_start:row_end],
                preferred_element_type=jnp.float32,
            )
            * score_scale
        )
        d_values = d_values.at[:row_end].add(
            jnp.einsum("jgqk,qjgd->kjd", attn_probs, d_block, preferred_element_type=jnp.float32)
        )
    d_queries = rotate_back(
        jnp.concatenate(d_query_blocks, axis=0),
        cosine[:, None, None, :],
        sine_table[:, None, None, :],
    )
    d_keys = rotate_back(d_keys, cosine[:, None, :], sine_table[:, None, :])
    d_proj = jnp.concatenate(
        [
            d_queries.reshape(group_rows, query_columns),
            d_keys.reshape(group_rows, key_columns),
            d_values.reshape(group_rows, key_columns),
        ],
        axis=1,
    ).astype(jnp.bfloat16)
    d_proj, up_sum, down_sum, gate_sum = after(d_proj, up_sum, down_sum, gate_sum)
    qkv_grad = contract_rows(normed_one, d_proj).astype(jnp.bfloat16)
    bias_grad = jnp.sum(d_proj, axis=0, dtype=jnp.float32)
    d_normed_one = sum_pair(lambda t: times_transpose(half_rows(d_proj, t), qkv_weight))
    d_token_norm, gain_one_grad = rms_backward(token_vals, rms_one, norm1_gain, d_normed_one)
    tokens_grad = d_hidden + d_token_norm
    up_grad = dp_rest(up_sum, bits_x, 2)
    down_grad = dp_rest(down_sum, bits_x, 3).T
    gate_grad = dp_rest(gate_sum, bits_z, 3)
    width = norm1_gain.shape[0]
    count = lax.axis_size("dp")
    share = width // count
    bias_columns = bias_grad.shape[0]
    values = jnp.concatenate([gain_one_grad, gain_two_grad, bias_grad]).astype(jnp.bfloat16)
    lanes = -(-values.shape[0] // (share * 128)) * 128
    values = jnp.pad(values, (0, share * lanes - values.shape[0])).reshape(1, share, lanes)
    values = jnp.broadcast_to(values, (count, share, lanes))
    small = jnp.concatenate([dp_blocks(qkv_grad), dp_blocks(out_grad), values], axis=2)
    small = dp_rest(small, bits_x, 0)
    columns = qkv_weight.shape[1]
    qkv_grad = small[:, :columns]
    out_grad = small[:, columns : columns + query_columns].T
    sums = small[:, columns + query_columns :].reshape(-1)
    gain_at = lax.axis_index("dp") * share
    gain_mine = jnp.concatenate(
        [
            lax.dynamic_slice_in_dim(sums, gain_at, share),
            lax.dynamic_slice_in_dim(sums, width + gain_at, share),
        ]
    )
    gain_mine = gain_mine + pair_swap(gain_mine)
    gain_one_grad = gain_mine[:share]
    gain_two_grad = gain_mine[share:]
    bias_grad = sums[2 * width : 2 * width + bias_columns]
    return (
        block_result,
        tokens_grad,
        gain_one_grad,
        qkv_grad,
        bias_grad,
        out_grad,
        gain_two_grad,
        gate_grad,
        up_grad,
        down_grad,
    )


def solution(mesh):
    in_specs = (
        P(("dp", "tensor"), None),
        P(("dp", "tensor"), None),
        P(),
        P(),
        P(),
        P(None, "tensor"),
        P("tensor"),
        P("tensor", None),
        P(),
        P(None, "tensor"),
        P(None, "tensor"),
        P("tensor", None),
    )
    out_specs = (
        P(("dp", "tensor"), None),
        P(("dp", "tensor"), None),
        P("dp"),
        P("dp", "tensor"),
        P("tensor"),
        P("tensor", "dp"),
        P("dp"),
        P("dp", "tensor"),
        P("dp", "tensor"),
        P("tensor", "dp"),
    )
    return jax.shard_map(shards, mesh=mesh, in_specs=in_specs, out_specs=out_specs, check_vma=False)
```

```python
import jax
import jax.numpy as jnp
from jax import lax
from jax.sharding import PartitionSpec as P

QUERY_HEADS = 14
KEY_VALUE_HEADS = 2
HEAD_WIDTH = 64
SEQ_DEV = 4
QB = 512


norm_eps = 1e-06
rope_base = 1000000.0
masked_score = -1e30


def seq_layout(lengths, placed, group_id, number_of_slots):
    target = group_id * SEQ_DEV + jnp.arange(SEQ_DEV, dtype=jnp.int32)
    owned = placed[None, :] == target[:, None]
    counted = jnp.sum(jnp.where(owned, lengths[None, :], 0), axis=1)
    seq_ends = jnp.cumsum(counted)
    seq_starts = seq_ends - counted
    slot_ids = jnp.arange(number_of_slots, dtype=jnp.int32)
    inside = (slot_ids[:, None] >= seq_starts[None, :]) & (slot_ids[:, None] < seq_ends[None, :])
    ranks = jnp.arange(SEQ_DEV, dtype=jnp.int32)
    segment = jnp.sum(jnp.where(inside, ranks[None, :], 0), axis=1) + jnp.where(
        jnp.any(inside, axis=1), 0, SEQ_DEV
    )
    position = slot_ids - jnp.sum(jnp.where(inside, seq_starts[None, :], 0), axis=1)
    return (segment, position)


def rope_tables(position):
    half_dim = HEAD_WIDTH // 2
    inverse = jnp.power(rope_base, -2.0 * jnp.arange(half_dim, dtype=jnp.float32) / HEAD_WIDTH)
    angles = position.astype(jnp.float32)[:, None] * inverse[None, :]
    return (jnp.cos(angles), jnp.sin(angles))


def rotate(vectors, cosine, sine_table):
    half_dim = vectors.shape[-1] // 2
    first_half = vectors[..., :half_dim]
    second_half = vectors[..., half_dim:]
    return jnp.concatenate(
        [
            first_half * cosine - second_half * sine_table,
            second_half * cosine + first_half * sine_table,
        ],
        axis=-1,
    )


def rotate_back(vectors, cosine, sine_table):
    half_dim = vectors.shape[-1] // 2
    first_half = vectors[..., :half_dim]
    second_half = vectors[..., half_dim:]
    return jnp.concatenate(
        [
            first_half * cosine + second_half * sine_table,
            second_half * cosine - first_half * sine_table,
        ],
        axis=-1,
    )


def allowed_keys(segment, row_start, row_end):
    query_ids = jnp.arange(row_start, row_end, dtype=jnp.int32)
    key_ids = jnp.arange(0, row_end, dtype=jnp.int32)
    query_seg = segment[row_start:row_end]
    same = query_seg[:, None] == segment[None, :row_end]
    causal = key_ids[None, :] <= query_ids[:, None]
    real_row = (query_seg[:, None] < SEQ_DEV) | (key_ids[None, :] == query_ids[:, None])
    return same & causal & real_row


def rms_forward(token_rows, gain):
    rms_scale = lax.rsqrt(jnp.mean(token_rows * token_rows, axis=-1, keepdims=True) + norm_eps)
    return (rms_scale, token_rows * rms_scale * gain)


def rms_backward(token_rows, rms_scale, gain, grad_rows):
    weighted = gain * grad_rows
    inner = jnp.mean(weighted * token_rows, axis=-1, keepdims=True)
    row_grad = rms_scale * weighted - token_rows * (rms_scale * rms_scale * rms_scale) * inner
    gain_grad = jnp.sum(grad_rows * token_rows * rms_scale, axis=0)
    return (row_grad, gain_grad)


def contract_rows(left, right):
    return lax.dot_general(
        left, right, (((0,), (0,)), ((), ())), preferred_element_type=jnp.float32
    )


def times_transpose(left, right):
    return lax.dot_general(
        left, right, (((1,), (1,)), ((), ())), preferred_element_type=jnp.float32
    )


def pair_swap(block):
    return lax.ppermute(block, "tensor", [(0, 1), (1, 0)])


def gather_pair(own):
    other = pair_swap(own)
    first = lax.axis_index("tensor") == 0
    return jnp.concatenate(
        [jnp.where(first, own, other), jnp.where(first, other, own)], axis=0
    )


def half_rows(array, which):
    rows = array.shape[0] // 2
    return lax.dynamic_slice_in_dim(array, which * rows, rows, axis=0)


def sum_pair(partial_of):
    me = lax.axis_index("tensor")
    sent = pair_swap(partial_of(1 - me).astype(jnp.bfloat16))
    return partial_of(me) + sent.astype(jnp.float32)


def dp_bits(last_first):
    count = lax.axis_size("dp")
    bits = []
    step = 1
    while step < count:
        bits.append(step)
        step *= 2
    if last_first:
        bits = bits[:1] + bits[2:] + bits[1:2]
    return bits


def dp_blocks(partial):
    count = lax.axis_size("dp")
    return partial.reshape(count, partial.shape[0] // count, partial.shape[1])


def dp_stage(current, bits, at):
    count = lax.axis_size("dp")
    step = bits[at]
    low = 2 ** sum(1 for later in bits[at + 1 :] if later < step)
    blocks, rows, columns = current.shape
    bit = (lax.axis_index("dp") // step) % 2
    pairs = current.reshape(blocks // (2 * low), 2, low, rows, columns)
    sent = lax.dynamic_index_in_dim(pairs, 1 - bit, axis=1, keepdims=False)
    kept = lax.dynamic_index_in_dim(pairs, bit, axis=1, keepdims=False)
    sent = sent.reshape(blocks // 2, rows, columns)
    kept = kept.reshape(blocks // 2, rows, columns)
    got = lax.ppermute(sent, "dp", [(i, i ^ step) for i in range(count)])
    total = kept.astype(jnp.float32) + got.astype(jnp.float32)
    return total if at == len(bits) - 1 else total.astype(jnp.bfloat16)


def dp_rest(current, bits, at):
    while at < len(bits):
        current = dp_stage(current, bits, at)
        at += 1
    return current[0]


def after(value, *earlier):
    return lax.optimization_barrier((value,) + earlier)


def shards(
    tokens,
    cotangent,
    seq_lengths,
    seq_place,
    norm1_gain,
    qkv_weight,
    qkv_bias,
    out_weight,
    norm2_gain,
    gate_weight,
    up_weight,
    down_weight,
):
    local_rows = tokens.shape[0]
    group_rows = local_rows * lax.axis_size("tensor")
    segment, position = seq_layout(seq_lengths, seq_place, lax.axis_index("dp"), group_rows)
    query_columns = out_weight.shape[0]
    key_columns = (qkv_weight.shape[1] - query_columns) // 2
    kv_local = key_columns // HEAD_WIDTH
    heads_per_group = QUERY_HEADS // KEY_VALUE_HEADS
    score_scale = HEAD_WIDTH ** (-0.5)
    block_count = group_rows // QB
    token_vals = tokens.astype(jnp.float32)
    rms_one, normed_one = rms_forward(token_vals, norm1_gain)
    normed_one = gather_pair(normed_one.astype(jnp.bfloat16))
    projected = jnp.dot(normed_one, qkv_weight, preferred_element_type=jnp.float32) + qkv_bias
    query_rows = projected[:, :query_columns].reshape(
        group_rows, kv_local, heads_per_group, HEAD_WIDTH
    )
    key_matrix = projected[:, query_columns : query_columns + key_columns].reshape(
        group_rows, kv_local, HEAD_WIDTH
    )
    value_matrix = (
        projected[:, query_columns + key_columns :]
        .reshape(group_rows, kv_local, HEAD_WIDTH)
        .astype(jnp.bfloat16)
    )
    cosine, sine_table = rope_tables(position)
    queries_r = rotate(query_rows, cosine[:, None, None, :], sine_table[:, None, None, :]).astype(
        jnp.bfloat16
    )
    keys_r = rotate(key_matrix, cosine[:, None, :], sine_table[:, None, :]).astype(jnp.bfloat16)
    key_masks = []
    log_totals = []
    contexts = []
    for block_id in range(block_count):
        row_start = block_id * QB
        row_end = row_start + QB
        key_mask = allowed_keys(segment, row_start, row_end)
        scores = (
            jnp.einsum(
                "qjgd,kjd->jgqk",
                queries_r[row_start:row_end],
                keys_r[:row_end],
                preferred_element_type=jnp.float32,
            )
            * score_scale
        )
        scores = jnp.where(key_mask[None, None], scores, masked_score)
        row_max = jnp.max(scores, axis=-1, keepdims=True)
        expo = jnp.exp(scores - row_max)
        row_total = jnp.sum(expo, axis=-1, keepdims=True)
        attn_probs = (expo / row_total).astype(jnp.bfloat16)
        key_masks.append(key_mask)
        log_totals.append(row_max + jnp.log(row_total))
        contexts.append(
            jnp.einsum(
                "jgqk,kjd->qjgd",
                attn_probs,
                value_matrix[:row_end],
                preferred_element_type=jnp.float32,
            )
        )
    context = (
        jnp.concatenate(contexts, axis=0).reshape(group_rows, query_columns).astype(jnp.bfloat16)
    )
    cot_sent, _ = after(cotangent, contexts[0])
    cot_group = gather_pair(cot_sent)
    hidden_one = token_vals + sum_pair(
        lambda t: jnp.dot(half_rows(context, t), out_weight, preferred_element_type=jnp.float32)
    )
    rms_two, normed_two = rms_forward(hidden_one, norm2_gain)
    d_mixed = times_transpose(cot_group, down_weight)
    normed_two, d_mixed = after(gather_pair(normed_two.astype(jnp.bfloat16)), d_mixed)
    gate_pre = jnp.dot(normed_two, gate_weight, preferred_element_type=jnp.float32)
    up_pre = jnp.dot(normed_two, up_weight, preferred_element_type=jnp.float32)
    activated = jax.nn.silu(gate_pre)
    mixed = (activated * up_pre).astype(jnp.bfloat16)
    sigmoid_gate = jax.nn.sigmoid(gate_pre)
    d_gate = (d_mixed * up_pre * sigmoid_gate * (1.0 + gate_pre * (1.0 - sigmoid_gate))).astype(
        jnp.bfloat16
    )
    d_up = (d_mixed * activated).astype(jnp.bfloat16)
    me = lax.axis_index("tensor")
    other_part = (
        times_transpose(half_rows(d_gate, 1 - me), gate_weight)
        + times_transpose(half_rows(d_up, 1 - me), up_weight)
    ).astype(jnp.bfloat16)
    d_normed_sent = pair_swap(other_part)
    mixed, d_gate, d_up, other_part = after(mixed, d_gate, d_up, other_part)
    own_part = times_transpose(half_rows(d_gate, me), gate_weight) + times_transpose(
        half_rows(d_up, me), up_weight
    )
    down_grad = contract_rows(cot_group, mixed).astype(jnp.bfloat16)
    gate_grad = contract_rows(normed_two, d_gate).astype(jnp.bfloat16)
    own_part, d_normed_sent, down_grad, gate_grad = after(
        own_part, d_normed_sent, down_grad, gate_grad
    )
    d_normed_two = own_part + d_normed_sent.astype(jnp.float32)
    bits_x = dp_bits(False)
    bits_z = dp_bits(True)
    down_sum = dp_stage(dp_blocks(down_grad), bits_x, 0)
    gate_sum = dp_stage(dp_blocks(gate_grad), bits_z, 0)
    d_hidden_norm, gain_two_grad = rms_backward(hidden_one, rms_two, norm2_gain, d_normed_two)
    d_hidden = cotangent.astype(jnp.float32) + d_hidden_norm
    d_resid_own = d_hidden.astype(jnp.bfloat16)
    d_up, mixed, d_resid_own = after(d_up, mixed, d_resid_own)
    d_resid = gather_pair(d_resid_own)
    up_grad = contract_rows(normed_two, d_up).astype(jnp.bfloat16)
    block_sent = jnp.dot(
        half_rows(mixed, 1 - me), down_weight, preferred_element_type=jnp.float32
    ).astype(jnp.bfloat16)
    block_own = jnp.dot(half_rows(mixed, me), down_weight, preferred_element_type=jnp.float32)
    d_resid, up_grad, block_sent, block_own, down_sum, gate_sum = after(
        d_resid, up_grad, block_sent, block_own, down_sum, gate_sum
    )
    up_sum = dp_stage(dp_blocks(up_grad), bits_x, 0)
    down_sum = dp_stage(down_sum, bits_x, 1)
    gate_sum = dp_stage(gate_sum, bits_z, 1)
    block_result = (hidden_one + (block_own + pair_swap(block_sent).astype(jnp.float32))).astype(
        jnp.bfloat16
    )
    out_grad = contract_rows(d_resid, context).astype(jnp.bfloat16)
    d_context = (
        times_transpose(d_resid, out_weight)
        .astype(jnp.bfloat16)
        .reshape(group_rows, kv_local, heads_per_group, HEAD_WIDTH)
    )
    d_query_blocks = []
    d_keys = jnp.zeros((group_rows, kv_local, HEAD_WIDTH), jnp.float32)
    d_values = jnp.zeros((group_rows, kv_local, HEAD_WIDTH), jnp.float32)
    for block_id in range(block_count):
        row_start = block_id * QB
        row_end = row_start + QB
        scores = (
            jnp.einsum(
                "qjgd,kjd->jgqk",
                queries_r[row_start:row_end],
                keys_r[:row_end],
                preferred_element_type=jnp.float32,
            )
            * score_scale
        )
        scores = jnp.where(key_masks[block_id][None, None], scores, masked_score)
        probs_full = jnp.exp(scores - log_totals[block_id])
        attn_probs = probs_full.astype(jnp.bfloat16)
        d_block = d_context[row_start:row_end]
        d_probs = jnp.einsum(
            "qjgd,kjd->jgqk", d_block, value_matrix[:row_end], preferred_element_type=jnp.float32
        )
        inner = jnp.sum(probs_full * d_probs, axis=-1, keepdims=True)
        d_scores = (probs_full * (d_probs - inner)).astype(jnp.bfloat16)
        d_query_blocks.append(
            jnp.einsum(
                "jgqk,kjd->qjgd", d_scores, keys_r[:row_end], preferred_element_type=jnp.float32
            )
            * score_scale
        )
        if block_id == 0:
            d_scores, d_context, up_sum, down_sum, gate_sum, block_result = after(
                d_scores, d_context, up_sum, down_sum, gate_sum, block_result
            )
            up_sum = dp_stage(up_sum, bits_x, 1)
            down_sum = dp_stage(down_sum, bits_x, 2)
            gate_sum = dp_stage(gate_sum, bits_z, 2)
        d_keys = d_keys.at[:row_end].add(
            jnp.einsum(
                "jgqk,qjgd->kjd",
                d_scores,
                queries_r[row_start:row_end],
                preferred_element_type=jnp.float32,
            )
            * score_scale
        )
        d_values = d_values.at[:row_end].add(
            jnp.einsum("jgqk,qjgd->kjd", attn_probs, d_block, preferred_element_type=jnp.float32)
        )
    d_queries = rotate_back(
        jnp.concatenate(d_query_blocks, axis=0),
        cosine[:, None, None, :],
        sine_table[:, None, None, :],
    )
    d_keys = rotate_back(d_keys, cosine[:, None, :], sine_table[:, None, :])
    d_proj = jnp.concatenate(
        [
            d_queries.reshape(group_rows, query_columns),
            d_keys.reshape(group_rows, key_columns),
            d_values.reshape(group_rows, key_columns),
        ],
        axis=1,
    ).astype(jnp.bfloat16)
    d_proj, up_sum, down_sum, gate_sum = after(d_proj, up_sum, down_sum, gate_sum)
    qkv_grad = contract_rows(normed_one, d_proj).astype(jnp.bfloat16)
    bias_grad = jnp.sum(d_proj, axis=0, dtype=jnp.float32)
    d_normed_one = sum_pair(lambda t: times_transpose(half_rows(d_proj, t), qkv_weight))
    d_token_norm, gain_one_grad = rms_backward(token_vals, rms_one, norm1_gain, d_normed_one)
    tokens_grad = d_hidden + d_token_norm
    up_grad = dp_rest(up_sum, bits_x, 2)
    down_grad = dp_rest(down_sum, bits_x, 3).T
    gate_grad = dp_rest(gate_sum, bits_z, 3)
    width = norm1_gain.shape[0]
    count = lax.axis_size("dp")
    share = width // count
    bias_columns = bias_grad.shape[0]
    values = jnp.concatenate([gain_one_grad, gain_two_grad, bias_grad]).astype(jnp.bfloat16)
    lanes = -(-values.shape[0] // (share * 128)) * 128
    values = jnp.pad(values, (0, share * lanes - values.shape[0])).reshape(1, share, lanes)
    values = jnp.broadcast_to(values, (count, share, lanes))
    small = jnp.concatenate([dp_blocks(qkv_grad), dp_blocks(out_grad), values], axis=2)
    small = dp_rest(small, bits_x, 0)
    columns = qkv_weight.shape[1]
    qkv_grad = small[:, :columns]
    out_grad = small[:, columns : columns + query_columns].T
    sums = small[:, columns + query_columns :].reshape(-1)
    gain_at = lax.axis_index("dp") * share
    gain_mine = jnp.concatenate(
        [
            lax.dynamic_slice_in_dim(sums, gain_at, share),
            lax.dynamic_slice_in_dim(sums, width + gain_at, share),
        ]
    )
    gain_mine = gain_mine + pair_swap(gain_mine)
    gain_one_grad = gain_mine[:share]
    gain_two_grad = gain_mine[share:]
    bias_grad = sums[2 * width : 2 * width + bias_columns]
    return (
        block_result,
        tokens_grad,
        gain_one_grad,
        qkv_grad,
        bias_grad,
        out_grad,
        gain_two_grad,
        gate_grad,
        up_grad,
        down_grad,
    )


def solution(mesh):
    in_specs = (
        P(("dp", "tensor"), None),
        P(("dp", "tensor"), None),
        P(),
        P(),
        P(),
        P(None, "tensor"),
        P("tensor"),
        P("tensor", None),
        P(),
        P(None, "tensor"),
        P(None, "tensor"),
        P("tensor", None),
    )
    out_specs = (
        P(("dp", "tensor"), None),
        P(("dp", "tensor"), None),
        P("dp"),
        P("dp", "tensor"),
        P("tensor"),
        P("tensor", "dp"),
        P("dp"),
        P("dp", "tensor"),
        P("dp", "tensor"),
        P("tensor", "dp"),
    )
    return jax.shard_map(shards, mesh=mesh, in_specs=in_specs, out_specs=out_specs, check_vma=False)
```
